32 devices in a mesh: rep: 2 (over x), inter: 2 (over core), intra: 8 (over z, y).
Axes of the slice: x: 2, y: 2, z: 4, core: 2. Of those that a mesh axis runs over, the one named last changes fastest.
Arguments:
- inputs_saved: bfloat16 [4096, 7168], P(('rep', 'inter', 'intra')), parts along dimension 0, may hold values from -6 to 6
- out_grad: bfloat16 [4096, 7168], P(('rep', 'inter', 'intra')), parts along dimension 0, may hold values from -6 to 6
- expert_ids: int32 [4096, 8], P(('rep', 'inter', 'intra')), parts along dimension 0, may hold values from 0 to 255, all different within a row; in each aligned block of 128 rows (0 to 127, 128 to 255, ...) at most 4 rows name the same one
- routing_weights: bfloat16 [4096, 8], P(('rep', 'inter', 'intra')), parts along dimension 0, may hold values from 0.049804688 to 0.59765625
- w_gate: bfloat16 [16, 7168, 1024], P(('inter', 'intra')), may hold values from -0.0625 to 0.0625
- w_up: bfloat16 [16, 7168, 1024], P(('inter', 'intra')), may hold values from -0.0625 to 0.0625
- w_down: bfloat16 [16, 1024, 7168], P(('inter', 'intra')), may hold values from -0.125 to 0.125
Outputs:
- grad_input: bfloat16 [4096, 7168], P(('rep', 'inter', 'intra')), parts along dimension 0
The draws below stay inside these ranges and needn't reach their ends.
There are 2 independent parts, one for each index of `rep`. The reference program is written for one: setup_inputs(seed, part) draws one part's arguments, and reference() takes and returns one part's arrays. A program takes and returns all parts, laid end to end along the dimension named above; an argument that names none is the same for every part. Nothing has to cross between parts.
Inputs may be any that keep to these rules, and one draw needn't show every extreme that they name: `expert_ids`: each row names 8 different experts; within the rows of one device no expert is named more than 4 times, a bound that some block reaches; only experts below 8 contribute.
All inputs are finite; a program needn't handle non-finite values.
Results may differ from the reference program's by a relative error of at most 0.009.
Values may be sent and summed in bfloat16 or wider, within the bound.
A program may use at most 128 MiB of HBM per device.

```python
import math
import jax
import jax.numpy as jnp
import numpy as np
from jax import lax

D = 7168
FF = 2048
EXPERTS_ALL = 256
TOPK = 8
TOK_DEV = 128
MOST = 4
WIN = 8
SPLIT = 2
FF_DEV = 1024
TOKENS = 2048
N_INTER = 2
N_INTRA = 8


def shard_levels(own_key, shape, split, least, high):
    loudness, own = 1.0, jax.random.fold_in(own_key, 6)
    for dim, shards_of in split:
        draws = jnp.exp(jax.random.uniform(jax.random.fold_in(own, dim), (shards_of,), jnp.float32, least / len(split), high / len(split)))
        loudness = loudness * jnp.repeat(draws, shape[dim] // shards_of).reshape([-1 if axis == dim else 1 for axis in range(len(shape))])
    return loudness


def routed_block(key, own, number, rows, count, top, reach, slope):
    order = jax.random.permutation(key, count)
    crowded, ordinary = portions_of(count, rows * top, reach, slope, True), portions_of(count, rows * top, reach, slope, False)
    places = jnp.arange(count)

    def named(lengths, offset_by):
        used = int((lengths > 0).sum())
        fixed = max(1, used // 4)
        passed = fixed + (places - fixed + offset_by * (used - fixed)) % max(1, count - fixed)
        return jnp.zeros((count,), jnp.int32).at[order[jnp.where(places < fixed, places, passed)]].set(jnp.asarray(lengths, jnp.int32))

    lengths = jnp.where(number % 4 == 0, named(crowded, number // 4), named(ordinary, number - number // 4 - 1))
    mixed = jax.random.permutation(jax.random.fold_in(own, 3), count)
    giver, taker = mixed[0:count // 2 * 2:2], mixed[1:count // 2 * 2:2]
    margin = jnp.minimum(lengths[giver] - 1, reach - lengths[taker]) // 2
    margin = jnp.where((giver == order[0]) | (taker == order[0]) | (lengths[taker] == 0), 0, jnp.maximum(margin, 0))
    passed = jax.random.randint(jax.random.fold_in(own, 4), (count // 2,), 0, 1 << 20) % (margin + 1)
    lengths = lengths.at[giver].add(-passed).at[taker].add(passed)
    labels = jnp.searchsorted(jnp.cumsum(lengths), jnp.arange(rows * top), side="right").astype(jnp.int32)
    table = labels.reshape(top, rows).T
    table = table[jax.random.permutation(jax.random.fold_in(own, 1), rows)]
    offset_by = jax.random.randint(jax.random.fold_in(own, 2), (rows, 1), 0, top)
    return jnp.take_along_axis(table, (jnp.arange(top)[None, :] + offset_by) % top, axis=1)


def portions_of(number_of, total, most, skew, full):
    loads = [(1 << 20) // math.isqrt(grade ** skew) + 1 for grade in range(1, number_of + 1)]
    largest = most if full else min(most, max(-(-total // number_of), total * loads[0] // sum(loads)))
    least = 1 if total - largest >= number_of - 1 else 0
    holding, rest = [largest] + [least] * (number_of - 1), total - largest - least * (number_of - 1)
    while rest > 0:
        movable = [i for i in range(1, number_of) if holding[i] < largest] or [i for i in range(1, number_of) if holding[i] < most]
        pool, remaining = sum([loads[i] for i in movable]), rest
        for i in movable:
            extra = min(most - holding[i], max(1, remaining * loads[i] // pool), rest)
            holding[i] = holding[i] + extra
            rest = rest - extra
    return np.array(holding)


def normal_values(rng, dims, deviation, most, shards=(), kind=jnp.bfloat16):
    values = deviation * jax.random.normal(rng, dims, jnp.float32)
    if shards:
        values = values * shard_levels(rng, dims, shards, -0.22, 0.18)
    return jnp.clip(values, -most, most).astype(kind)


def setup_inputs(seed: int = 0, part: int = 0) -> dict:
    key_of = jax.random.split(jax.random.key(seed), 8)
    own_keys = jax.random.split(jax.random.fold_in(key_of[7], part), 8)
    inputs_saved = normal_values(own_keys[0], (TOKENS, D), 1.0, 6.0, ((0, 16),))
    out_grad = normal_values(own_keys[1], (TOKENS, D), 1.0, 6.0, ((0, 16),))
    expert_ids_keys = jax.random.split(jax.random.fold_in(own_keys[2], 1), TOKENS // TOK_DEV)
    expert_ids_turns = jax.random.permutation(jax.random.fold_in(own_keys[2], 3), TOKENS // TOK_DEV)
    expert_ids = jax.vmap(lambda own, number: routed_block(jax.random.fold_in(own_keys[2], 2), own, number, TOK_DEV, EXPERTS_ALL, TOPK, MOST, 1))(expert_ids_keys, expert_ids_turns).reshape((TOKENS, TOPK))
    routing_weights = jnp.clip(0.049804688 + 0.54785156 * jax.random.uniform(own_keys[3], (TOKENS, TOPK), jnp.float32) ** shard_levels(own_keys[3], (TOKENS, TOPK), ((0, 16),), -0.2, 0.2), 0.049804688, 0.59765625).astype(jnp.bfloat16)
    w_gate = normal_values(key_of[4], (WIN * SPLIT, D, FF_DEV), D ** -0.5, 0.0625, ((0, 16),))
    w_up = normal_values(key_of[5], (WIN * SPLIT, D, FF_DEV), D ** -0.5, 0.0625, ((0, 16),))
    w_down = normal_values(key_of[6], (WIN * SPLIT, FF_DEV, D), FF ** -0.5, 0.125, ((0, 16),))
    return dict(inputs_saved=inputs_saved, out_grad=out_grad, expert_ids=expert_ids, routing_weights=routing_weights, w_gate=w_gate, w_up=w_up, w_down=w_down)


def expert_partial(rows_x, rows_grad, scales, gate_full, up_full, down_full):
    gate_pre = jnp.dot(rows_x, gate_full, preferred_element_type=jnp.float32)
    up_pre = jnp.dot(rows_x, up_full, preferred_element_type=jnp.float32)
    hidden_raw = jnp.dot(rows_grad, down_full.T, preferred_element_type=jnp.float32)
    hidden_grad = scales[:, None] * hidden_raw
    sigmoid_gate = jax.nn.sigmoid(gate_pre)
    gate_grad = (hidden_grad * up_pre * sigmoid_gate * (1.0 + gate_pre * (1.0 - sigmoid_gate))).astype(jnp.bfloat16)
    up_grad = (hidden_grad * gate_pre * sigmoid_gate).astype(jnp.bfloat16)
    row_count = rows_x.shape[0]
    gate_blocks = gate_grad.reshape(row_count, SPLIT, FF_DEV).astype(jnp.float32)
    up_blocks = up_grad.reshape(row_count, SPLIT, FF_DEV).astype(jnp.float32)
    gate_mats = gate_full.reshape(D, SPLIT, FF_DEV).astype(jnp.float32)
    up_mats = up_full.reshape(D, SPLIT, FF_DEV).astype(jnp.float32)
    partial_rows = jnp.einsum("rsh,dsh->rsd", gate_blocks, gate_mats) + jnp.einsum("rsh,dsh->rsd", up_blocks, up_mats)
    partial_rows = partial_rows.astype(jnp.bfloat16).astype(jnp.float32)
    return jnp.sum(partial_rows, axis=1)


def reference(inputs_saved, out_grad, expert_ids, routing_weights, w_gate, w_up, w_down):
    pair_count = TOKENS * TOPK
    capacity = N_INTER * N_INTRA * MOST
    pair_experts = expert_ids.reshape(-1)
    pair_scales = routing_weights.reshape(-1).astype(jnp.float32)
    positions = jnp.arange(pair_count, dtype=jnp.int32)

    def one_expert(total, expert_index):
        sort_key = jnp.where(pair_experts == expert_index, positions, pair_count + positions)
        ordering = jnp.argsort(sort_key)[:capacity].astype(jnp.int32)
        is_valid = sort_key[ordering] < pair_count
        token_of = (ordering // TOPK).astype(jnp.int32)
        scales = jnp.where(is_valid, pair_scales[ordering], 0.0)
        start = (expert_index * SPLIT).astype(jnp.int32)
        gate_full = lax.dynamic_slice_in_dim(w_gate, start, SPLIT, 0).transpose(1, 0, 2).reshape(D, FF)
        up_full = lax.dynamic_slice_in_dim(w_up, start, SPLIT, 0).transpose(1, 0, 2).reshape(D, FF)
        down_full = lax.dynamic_slice_in_dim(w_down, start, SPLIT, 0).reshape(FF, D)
        contrib = expert_partial(inputs_saved[token_of], out_grad[token_of], scales, gate_full, up_full, down_full)
        contrib = jnp.where(is_valid[:, None], contrib, 0.0)
        return total.at[token_of].add(contrib), None

    initial = jnp.zeros((TOKENS, D), jnp.float32)
    total, unused = lax.scan(one_expert, initial, jnp.arange(WIN, dtype=jnp.int32))
    return total.astype(jnp.bfloat16)
```

```python
import functools

import jax
import jax.numpy as jnp
from jax import lax
from jax.experimental import pallas as pl
from jax.experimental.pallas import tpu as pltpu
from jax.sharding import PartitionSpec as P

EG = 4
MOST = 4
KD = 7
KR = 7


def expert_rows(rows_x, rows_grad, scales, gate_mat, up_mat, down_mat):
    gate_pre = jnp.dot(rows_x, gate_mat, preferred_element_type=jnp.float32)
    up_pre = jnp.dot(rows_x, up_mat, preferred_element_type=jnp.float32)
    hidden_raw = lax.dot_general(
        rows_grad, down_mat, (((1,), (1,)), ((), ())), preferred_element_type=jnp.float32
    )
    hidden_grad = scales.astype(jnp.float32)[:, None] * hidden_raw
    sigmoid_gate = jax.nn.sigmoid(gate_pre)
    gate_grad = (
        hidden_grad * up_pre * sigmoid_gate * (1.0 + gate_pre * (1.0 - sigmoid_gate))
    ).astype(jnp.bfloat16)
    up_grad = (hidden_grad * gate_pre * sigmoid_gate).astype(jnp.bfloat16)
    contract = (((1,), (1,)), ((), ()))
    result = lax.dot_general(gate_grad, gate_mat, contract, preferred_element_type=jnp.float32)
    result = result + lax.dot_general(up_grad, up_mat, contract, preferred_element_type=jnp.float32)
    return result.astype(jnp.bfloat16)


def on_device(inputs_saved, out_grad, expert_ids, routing_weights, w_gate, w_up, w_down):
    n_inter = lax.axis_size("inter")
    n_intra = lax.axis_size("intra")
    shard_count = n_intra // EG
    window = n_inter * EG
    width = inputs_saved.shape[1]
    token_count = inputs_saved.shape[0]
    top_count = expert_ids.shape[1]
    slot_count = MOST
    gate_mat = w_gate[0]
    up_mat = w_up[0]
    down_mat = w_down[0]
    pair_experts = expert_ids.reshape(-1)
    onehot = (pair_experts[:, None] == jnp.arange(window, dtype=jnp.int32)[None, :]).astype(
        jnp.int32
    )
    slot_rank = jnp.cumsum(onehot, axis=0) - 1
    select = onehot[None, :, :] * (
        slot_rank[None, :, :] == jnp.arange(slot_count, dtype=jnp.int32)[:, None, None]
    ).astype(jnp.int32)
    per_token = select.reshape(slot_count, token_count, top_count, window).sum(axis=2)
    chosen = per_token.transpose(2, 0, 1).reshape(window * slot_count, token_count)
    chosen_bf = chosen.astype(jnp.bfloat16)
    x_buffer = (
        jnp.dot(chosen_bf, inputs_saved, preferred_element_type=jnp.float32)
        .astype(jnp.bfloat16)
        .reshape(window, slot_count, width)
    )
    grad_buffer = (
        jnp.dot(chosen_bf, out_grad, preferred_element_type=jnp.float32)
        .astype(jnp.bfloat16)
        .reshape(window, slot_count, width)
    )
    scale_sum = jnp.sum(
        select.astype(jnp.float32) * routing_weights.reshape(-1).astype(jnp.float32)[None, :, None],
        axis=1,
    )
    scale_buffer = scale_sum.transpose(1, 0).astype(jnp.bfloat16)
    outbox = (
        jnp.repeat(x_buffer, shard_count, axis=0),
        jnp.repeat(grad_buffer, shard_count, axis=0),
        jnp.repeat(scale_buffer, shard_count, axis=0),
    )
    rows_x = lax.all_to_all(outbox[0], ("inter", "intra"), split_axis=0, concat_axis=0, tiled=True)
    leading = rows_x.shape[:-1]
    result = expert_rows(
        rows_x.reshape(-1, width),
        lax.all_to_all(
            outbox[1], ("inter", "intra"), split_axis=0, concat_axis=0, tiled=True
        ).reshape(-1, width),
        lax.all_to_all(
            outbox[2], ("inter", "intra"), split_axis=0, concat_axis=0, tiled=True
        ).reshape(-1),
        gate_mat,
        up_mat,
        down_mat,
    )
    partial_rows = result.reshape(leading + (width,))
    returned = lax.all_to_all(
        partial_rows, ("inter", "intra"), split_axis=0, concat_axis=0, tiled=True
    )
    summed = (
        returned.astype(jnp.float32).reshape(window, shard_count, slot_count, width).sum(axis=1)
    )
    gathered = jnp.dot(
        chosen.astype(jnp.float32).T,
        summed.reshape(window * slot_count, width),
        precision=lax.Precision.HIGHEST,
        preferred_element_type=jnp.float32,
    )
    return gathered.astype(jnp.bfloat16)


MESH = pl.DeviceIdType.MESH
BF = jnp.bfloat16
F32 = jnp.float32
EXPERTS = 8
NT = (((1,), (1,)), ((), ()))


def iota(shape, dim):
    return lax.broadcasted_iota(jnp.int32, shape, dim)


def fused_kernel(
    kd, kr, x_ref, g_ref, ids_ref, rw_ref, wg_hbm, wu_hbm, wd_hbm, out_ref,
    wg, wu, wd, outbox, rin, acc_g, acc_u, acc_h, gg, uu, own, pout, pin, rout, rret,
    select, coef, perm, perm_back,
    w_sem, send_sem, recv_sem, fsend, frecv, psend, precv, rsend, rrecv,
):
    tokens, width = x_ref.shape
    half, quarter = width // 2, width // 4
    cw, qw = half // kd, quarter // kr
    rep, core, pos = lax.axis_index("rep"), lax.axis_index("inter"), lax.axis_index("intra")
    z, y = pos // 2, pos % 2
    me = core * EG + z
    partner = (rep, core, z * 2 + 1 - y)

    def peer(e):
        return (rep, e // EG, (e % EG) * 2 + y)

    barrier = pltpu.get_barrier_semaphore()
    for d in range(1, EXPERTS):
        pl.semaphore_signal(barrier, inc=1, device_id=peer((me + d) % EXPERTS), device_id_type=MESH)
    pl.semaphore_signal(barrier, inc=1, device_id=partner, device_id_type=MESH)

    def cols(k, h):
        return pl.ds(pl.multiple_of(h * half + k * cw, 128), cw)

    def qcols(k, q):
        return pl.ds(pl.multiple_of(q * quarter + k * qw, 128), qw)

    def weight_copies(k):
        res = []
        for h in range(2):
            c = cols(k, h)
            res.append(pltpu.make_async_copy(wg_hbm.at[0, c, :], wg.at[c, :], w_sem.at[0, k, h]))
            res.append(pltpu.make_async_copy(wu_hbm.at[0, c, :], wu.at[c, :], w_sem.at[1, k, h]))
            res.append(pltpu.make_async_copy(wd_hbm.at[0, :, c], wd.at[:, c], w_sem.at[2, k, h]))
        return res

    @pl.loop(0, kd)
    def _(k):
        for copy in weight_copies(k):
            copy.start()

    n = EXPERTS * 16
    col = iota((tokens, n), 1)
    expert, place = col // 16, col % 4
    present = jnp.zeros((tokens, n), F32)
    weight = jnp.zeros((tokens, n), F32)
    ids = ids_ref[...]
    rw = rw_ref[...].astype(F32)
    for t in range(ids.shape[1]):
        hit = (ids[:, t : t + 1] == expert).astype(F32)
        present = present + hit
        weight = weight + hit * rw[:, t : t + 1]
    lower = (iota((tokens, tokens), 1) < iota((tokens, tokens), 0)).astype(F32).astype(BF)
    rank = jnp.dot(lower, present.astype(BF), preferred_element_type=F32)
    chosen = jnp.where(rank == place.astype(F32), present, 0.0)
    coef_all = chosen * weight
    for q in range(4):
        coef[q] = jnp.where((col % 16) // 4 == q, coef_all, 0.0).astype(BF)
    chosen_t = chosen.T
    row = iota((n, tokens), 0)
    for j in range(4):
        select[j] = jnp.where((row % 16) // 4 == j, chosen_t, 0.0).astype(BF)
    o, c = iota((2 * n, 2 * n), 0), iota((2 * n, 2 * n), 1)
    source = ((o // 32) % 2) * 128 + ((o // 4) % 8) * 16 + (o // 128) * 8 + ((o // 64) % 2) * 4 + o % 4
    perm[...] = (c == source).astype(F32).astype(BF)
    o, c = iota((n, n), 0), iota((n, n), 1)
    perm_back[...] = (c == ((o // 4) % 4) * 32 + (o // 16) * 4 + o % 4).astype(F32).astype(BF)

    acc_g[...] = jnp.zeros_like(acc_g)
    acc_u[...] = jnp.zeros_like(acc_u)
    acc_h[...] = jnp.zeros_like(acc_h)

    def dispatch(k, e, slot):
        return pltpu.make_async_remote_copy(
            src_ref=outbox.at[k, e], dst_ref=rin.at[k, 0, slot],
            send_sem=send_sem.at[k, e], recv_sem=recv_sem.at[k, slot],
            device_id=peer(e), device_id_type=MESH,
        )

    def forward(k):
        return pltpu.make_async_remote_copy(
            src_ref=rin.at[k, 0], dst_ref=rin.at[k, 1],
            send_sem=fsend.at[k], recv_sem=frecv.at[k],
            device_id=partner, device_id_type=MESH,
        )

    def exchange(k):
        return pltpu.make_async_remote_copy(
            src_ref=pout.at[k], dst_ref=pin.at[k],
            send_sem=psend.at[k], recv_sem=precv.at[k],
            device_id=partner, device_id_type=MESH,
        )

    def giveback(k, e, slot):
        return pltpu.make_async_remote_copy(
            src_ref=rout.at[k, e], dst_ref=rret.at[k, slot],
            send_sem=rsend.at[k, e], recv_sem=rrecv.at[k, slot],
            device_id=peer(e), device_id_type=MESH,
        )

    pl.semaphore_wait(barrier, EXPERTS)

    @pl.loop(0, kd)
    def _(k):
        msg = jnp.dot(select[0], x_ref[:, cols(k, 0)], preferred_element_type=F32)
        msg = msg + jnp.dot(select[1], g_ref[:, cols(k, 0)], preferred_element_type=F32)
        msg = msg + jnp.dot(select[2], x_ref[:, cols(k, 1)], preferred_element_type=F32)
        msg = msg + jnp.dot(select[3], g_ref[:, cols(k, 1)], preferred_element_type=F32)
        outbox[k] = msg.astype(BF).reshape(EXPERTS, 16, cw)
        for d in range(1, EXPERTS):
            dispatch(k, (me + d) % EXPERTS, me).start()
        rin[k, 0, me] = outbox[k, me]

    @pl.loop(0, kd + 1)
    def _(step):
        @pl.when(step < kd)
        def _():
            for d in range(1, EXPERTS):
                p = (me + d) % EXPERTS
                dispatch(step, p, p).wait_recv()
            forward(step).start()

        @pl.when(step >= 1)
        def _():
            k = step - 1
            for copy in weight_copies(k):
                copy.wait()
            forward(k).wait_recv()
            rows = jnp.dot(
                perm[...], rin[k].reshape(2 * n, cw), preferred_element_type=F32
            ).astype(BF)
            for h in range(2):
                xs = rows[h * 128 : h * 128 + 64]
                gs = rows[h * 128 + 64 : h * 128 + 128]
                acc_g[...] += jnp.dot(xs, wg[cols(k, h), :], preferred_element_type=F32)
                acc_u[...] += jnp.dot(xs, wu[cols(k, h), :], preferred_element_type=F32)
                acc_h[...] += lax.dot_general(gs, wd[:, cols(k, h)], NT, preferred_element_type=F32)

    gate, up, hidden = acc_g[...], acc_u[...], acc_h[...]
    sig = jax.nn.sigmoid(gate)
    gg[...] = (hidden * up * sig * (1.0 + gate * (1.0 - sig))).astype(BF)
    uu[...] = (hidden * gate * sig).astype(BF)

    @pl.loop(0, kr + 2)
    def _(step):
        @pl.when(step < kr)
        def _():
            for q in range(4):
                part = lax.dot_general(gg[...], wg[qcols(step, q), :], NT, preferred_element_type=F32)
                part = part + lax.dot_general(
                    uu[...], wu[qcols(step, q), :], NT, preferred_element_type=F32
                )
                own[step, q * 32 : (q + 1) * 32, :] = part[:32]
                pout[step, q * 32 : (q + 1) * 32, :] = part[32:].astype(BF)
            exchange(step).start()

        @pl.when((step >= 1) & (step < kr + 1))
        def _():
            k = step - 1
            exchange(k).wait_recv()
            total = (own[k] + pin[k].astype(F32)).astype(BF)
            rout[k] = (
                jnp.dot(perm_back[...], total, preferred_element_type=F32)
                .astype(BF)
                .reshape(EXPERTS, 16, qw)
            )
            for d in range(1, EXPERTS):
                giveback(k, (me + d) % EXPERTS, me).start()
            rret[k, me] = rout[k, me]

        @pl.when(step >= 2)
        def _():
            k = step - 2
            for d in range(1, EXPERTS):
                p = (me + d) % EXPERTS
                giveback(k, p, p).wait_recv()
            rows = rret[k].reshape(n, qw)
            for q in range(4):
                out_ref[:, qcols(k, q)] = jnp.dot(
                    coef[q], rows, preferred_element_type=F32
                ).astype(BF)

    @pl.loop(0, kd)
    def _(k):
        for d in range(1, EXPERTS):
            dispatch(k, (me + d) % EXPERTS, me).wait_send()
        forward(k).wait_send()

    @pl.loop(0, kr)
    def _(k):
        for d in range(1, EXPERTS):
            giveback(k, (me + d) % EXPERTS, me).wait_send()
        exchange(k).wait_send()


def fused(inputs_saved, out_grad, expert_ids, routing_weights, w_gate, w_up, w_down):
    tokens, width = inputs_saved.shape
    units = w_gate.shape[2]
    kd, kr = KD, KR
    cw, qw = width // 2 // kd, width // 4 // kr
    rows = 2 * EXPERTS * MOST
    n = EXPERTS * 16
    vmem = pl.BlockSpec(memory_space=pltpu.VMEM)
    hbm = pl.BlockSpec(memory_space=pl.ANY)
    dma = pltpu.SemaphoreType.DMA
    return pl.pallas_call(
        functools.partial(fused_kernel, kd, kr),
        out_shape=jax.ShapeDtypeStruct((tokens, width), BF),
        in_specs=[vmem] * 4 + [hbm] * 3,
        out_specs=vmem,
        scratch_shapes=[
            pltpu.VMEM((width, units), BF),
            pltpu.VMEM((width, units), BF),
            pltpu.VMEM((units, width), BF),
            pltpu.VMEM((kd, EXPERTS, 16, cw), BF),
            pltpu.VMEM((kd, 2, EXPERTS, 16, cw), BF),
            pltpu.VMEM((rows, units), F32),
            pltpu.VMEM((rows, units), F32),
            pltpu.VMEM((rows, units), F32),
            pltpu.VMEM((rows, units), BF),
            pltpu.VMEM((rows, units), BF),
            pltpu.VMEM((kr, n, qw), F32),
            pltpu.VMEM((kr, n, qw), BF),
            pltpu.VMEM((kr, n, qw), BF),
            pltpu.VMEM((kr, EXPERTS, 16, qw), BF),
            pltpu.VMEM((kr, EXPERTS, 16, qw), BF),
            pltpu.VMEM((4, n, tokens), BF),
            pltpu.VMEM((4, tokens, n), BF),
            pltpu.VMEM((2 * n, 2 * n), BF),
            pltpu.VMEM((n, n), BF),
            dma((3, kd, 2)),
            dma((kd, EXPERTS)),
            dma((kd, EXPERTS)),
            dma((kd,)),
            dma((kd,)),
            dma((kr,)),
            dma((kr,)),
            dma((kr, EXPERTS)),
            dma((kr, EXPERTS)),
        ],
        compiler_params=pltpu.CompilerParams(
            collective_id=0, has_side_effects=True, vmem_limit_bytes=62 * 1024 * 1024
        ),
    )(inputs_saved, out_grad, expert_ids, routing_weights, w_gate, w_up, w_down)


def fits(mesh, x_shape, w_shape):
    return (
        mesh.shape["inter"] == 2
        and mesh.shape["intra"] == 2 * EG
        and x_shape[1] % (256 * KD) == 0
        and x_shape[1] % (512 * KR) == 0
        and x_shape[0] == 128 * mesh.size
        and w_shape[2] <= 1024
    )


def solution(mesh):
    in_specs = (
        P(("rep", "inter", "intra"), None),
        P(("rep", "inter", "intra"), None),
        P(("rep", "inter", "intra"), None),
        P(("rep", "inter", "intra"), None),
        P(("inter", "intra"), None, None),
        P(("inter", "intra"), None, None),
        P(("inter", "intra"), None, None),
    )
    out_specs = P(("rep", "inter", "intra"), None)

    def run(*args):
        body = fused if fits(mesh, args[0].shape, args[4].shape) else on_device
        return jax.shard_map(
            body, mesh=mesh, in_specs=in_specs, out_specs=out_specs, check_vma=False
        )(*args)

    return run
```

```python
import functools

import jax
import jax.numpy as jnp
from jax import lax
from jax.experimental import pallas as pl
from jax.experimental.pallas import tpu as pltpu
from jax.sharding import PartitionSpec as P

EG = 4
MOST = 4
KD = 4
KR = 2


def expert_rows(rows_x, rows_grad, scales, gate_mat, up_mat, down_mat):
    gate_pre = jnp.dot(rows_x, gate_mat, preferred_element_type=jnp.float32)
    up_pre = jnp.dot(rows_x, up_mat, preferred_element_type=jnp.float32)
    hidden_raw = lax.dot_general(
        rows_grad, down_mat, (((1,), (1,)), ((), ())), preferred_element_type=jnp.float32
    )
    hidden_grad = scales.astype(jnp.float32)[:, None] * hidden_raw
    sigmoid_gate = jax.nn.sigmoid(gate_pre)
    gate_grad = (
        hidden_grad * up_pre * sigmoid_gate * (1.0 + gate_pre * (1.0 - sigmoid_gate))
    ).astype(jnp.bfloat16)
    up_grad = (hidden_grad * gate_pre * sigmoid_gate).astype(jnp.bfloat16)
    contract = (((1,), (1,)), ((), ()))
    result = lax.dot_general(gate_grad, gate_mat, contract, preferred_element_type=jnp.float32)
    result = result + lax.dot_general(up_grad, up_mat, contract, preferred_element_type=jnp.float32)
    return result.astype(jnp.bfloat16)


def on_device(inputs_saved, out_grad, expert_ids, routing_weights, w_gate, w_up, w_down):
    n_inter = lax.axis_size("inter")
    n_intra = lax.axis_size("intra")
    shard_count = n_intra // EG
    window = n_inter * EG
    width = inputs_saved.shape[1]
    token_count = inputs_saved.shape[0]
    top_count = expert_ids.shape[1]
    slot_count = MOST
    gate_mat = w_gate[0]
    up_mat = w_up[0]
    down_mat = w_down[0]
    pair_experts = expert_ids.reshape(-1)
    onehot = (pair_experts[:, None] == jnp.arange(window, dtype=jnp.int32)[None, :]).astype(
        jnp.int32
    )
    slot_rank = jnp.cumsum(onehot, axis=0) - 1
    select = onehot[None, :, :] * (
        slot_rank[None, :, :] == jnp.arange(slot_count, dtype=jnp.int32)[:, None, None]
    ).astype(jnp.int32)
    per_token = select.reshape(slot_count, token_count, top_count, window).sum(axis=2)
    chosen = per_token.transpose(2, 0, 1).reshape(window * slot_count, token_count)
    chosen_bf = chosen.astype(jnp.bfloat16)
    x_buffer = (
        jnp.dot(chosen_bf, inputs_saved, preferred_element_type=jnp.float32)
        .astype(jnp.bfloat16)
        .reshape(window, slot_count, width)
    )
    grad_buffer = (
        jnp.dot(chosen_bf, out_grad, preferred_element_type=jnp.float32)
        .astype(jnp.bfloat16)
        .reshape(window, slot_count, width)
    )
    scale_sum = jnp.sum(
        select.astype(jnp.float32) * routing_weights.reshape(-1).astype(jnp.float32)[None, :, None],
        axis=1,
    )
    scale_buffer = scale_sum.transpose(1, 0).astype(jnp.bfloat16)
    outbox = (
        jnp.repeat(x_buffer, shard_count, axis=0),
        jnp.repeat(grad_buffer, shard_count, axis=0),
        jnp.repeat(scale_buffer, shard_count, axis=0),
    )
    rows_x = lax.all_to_all(outbox[0], ("inter", "intra"), split_axis=0, concat_axis=0, tiled=True)
    leading = rows_x.shape[:-1]
    result = expert_rows(
        rows_x.reshape(-1, width),
        lax.all_to_all(
            outbox[1], ("inter", "intra"), split_axis=0, concat_axis=0, tiled=True
        ).reshape(-1, width),
        lax.all_to_all(
            outbox[2], ("inter", "intra"), split_axis=0, concat_axis=0, tiled=True
        ).reshape(-1),
        gate_mat,
        up_mat,
        down_mat,
    )
    partial_rows = result.reshape(leading + (width,))
    returned = lax.all_to_all(
        partial_rows, ("inter", "intra"), split_axis=0, concat_axis=0, tiled=True
    )
    summed = (
        returned.astype(jnp.float32).reshape(window, shard_count, slot_count, width).sum(axis=1)
    )
    gathered = jnp.dot(
        chosen.astype(jnp.float32).T,
        summed.reshape(window * slot_count, width),
        precision=lax.Precision.HIGHEST,
        preferred_element_type=jnp.float32,
    )
    return gathered.astype(jnp.bfloat16)


MESH = pl.DeviceIdType.MESH
BF = jnp.bfloat16
F32 = jnp.float32
EXPERTS = 8
NT = (((1,), (1,)), ((), ()))


def iota(shape, dim):
    return lax.broadcasted_iota(jnp.int32, shape, dim)


def fused_kernel(
    kd, kr, x_ref, g_ref, ids_ref, rw_ref, wg_hbm, wu_hbm, wd_hbm, out_ref,
    wg, wu, wd, outbox, rin, acc_g, acc_u, acc_h, gg, uu, own, pout, pin, rout, rret,
    select, coef, perm, perm_back,
    w_sem, send_sem, recv_sem, fsend, frecv, psend, precv, rsend, rrecv,
):
    tokens, width = x_ref.shape
    half, quarter = width // 2, width // 4
    cw, qw = half // kd, quarter // kr
    rep, core, pos = lax.axis_index("rep"), lax.axis_index("inter"), lax.axis_index("intra")
    z, y = pos // 2, pos % 2
    me = core * EG + z
    partner = (rep, core, z * 2 + 1 - y)

    def peer(e):
        return (rep, e // EG, (e % EG) * 2 + y)

    barrier = pltpu.get_barrier_semaphore()
    for d in range(1, EXPERTS):
        pl.semaphore_signal(barrier, inc=1, device_id=peer((me + d) % EXPERTS), device_id_type=MESH)
    pl.semaphore_signal(barrier, inc=1, device_id=partner, device_id_type=MESH)

    def cols(k, h):
        return pl.ds(pl.multiple_of(h * half + k * cw, 128), cw)

    def qcols(k, q):
        return pl.ds(pl.multiple_of(q * quarter + k * qw, 128), qw)

    def weight_copies(k):
        res = []
        for h in range(2):
            c = cols(k, h)
            res.append(pltpu.make_async_copy(wg_hbm.at[0, c, :], wg.at[c, :], w_sem.at[0, k, h]))
            res.append(pltpu.make_async_copy(wu_hbm.at[0, c, :], wu.at[c, :], w_sem.at[1, k, h]))
            res.append(pltpu.make_async_copy(wd_hbm.at[0, :, c], wd.at[:, c], w_sem.at[2, k, h]))
        return res

    @pl.loop(0, kd)
    def _(k):
        for copy in weight_copies(k):
            copy.start()

    n = EXPERTS * 16
    row = iota((n, tokens), 0)
    expert, place = row // 16, row % 4
    present = jnp.zeros((n, tokens), F32)
    weight = jnp.zeros((n, tokens), F32)
    ids = ids_ref[...]
    rw = rw_ref[...].astype(F32)
    for t in range(ids.shape[0]):
        hit = (ids[t : t + 1, :] == expert).astype(F32)
        present = present + hit
        weight = weight + hit * rw[t : t + 1, :]
    upper = (iota((tokens, tokens), 0) < iota((tokens, tokens), 1)).astype(F32).astype(BF)
    rank = jnp.dot(present.astype(BF), upper, preferred_element_type=F32)
    chosen = jnp.where(rank == place.astype(F32), present, 0.0)
    coef_all = (chosen * weight).T
    col = iota((tokens, n), 1)
    for q in range(4):
        coef[q] = jnp.where((col % 16) // 4 == q, coef_all, 0.0).astype(BF)
    for j in range(4):
        select[j] = jnp.where((row % 16) // 4 == j, chosen, 0.0).astype(BF)
    o, c = iota((2 * n, 2 * n), 0), iota((2 * n, 2 * n), 1)
    source = ((o // 32) % 2) * 128 + ((o // 4) % 8) * 16 + (o // 128) * 8 + ((o // 64) % 2) * 4 + o % 4
    perm[...] = (c == source).astype(F32).astype(BF)
    o, c = iota((n, n), 0), iota((n, n), 1)
    perm_back[...] = (c == ((o // 4) % 4) * 32 + (o // 16) * 4 + o % 4).astype(F32).astype(BF)

    acc_g[...] = jnp.zeros_like(acc_g)
    acc_u[...] = jnp.zeros_like(acc_u)
    acc_h[...] = jnp.zeros_like(acc_h)

    def dispatch(k, e, slot):
        return pltpu.make_async_remote_copy(
            src_ref=outbox.at[k, e], dst_ref=rin.at[k, 0, slot],
            send_sem=send_sem.at[k, e], recv_sem=recv_sem.at[k, slot],
            device_id=peer(e), device_id_type=MESH,
        )

    def forward(k):
        return pltpu.make_async_remote_copy(
            src_ref=rin.at[k, 0], dst_ref=rin.at[k, 1],
            send_sem=fsend.at[k], recv_sem=frecv.at[k],
            device_id=partner, device_id_type=MESH,
        )

    def exchange(k):
        return pltpu.make_async_remote_copy(
            src_ref=pout.at[k], dst_ref=pin.at[k],
            send_sem=psend.at[k], recv_sem=precv.at[k],
            device_id=partner, device_id_type=MESH,
        )

    def giveback(k, e, slot):
        return pltpu.make_async_remote_copy(
            src_ref=rout.at[k, e], dst_ref=rret.at[k, slot],
            send_sem=rsend.at[k, e], recv_sem=rrecv.at[k, slot],
            device_id=peer(e), device_id_type=MESH,
        )

    pl.semaphore_wait(barrier, EXPERTS)

    @pl.loop(0, kd)
    def _(k):
        msg = jnp.dot(select[0], x_ref[:, cols(k, 0)], preferred_element_type=F32)
        msg = msg + jnp.dot(select[1], g_ref[:, cols(k, 0)], preferred_element_type=F32)
        msg = msg + jnp.dot(select[2], x_ref[:, cols(k, 1)], preferred_element_type=F32)
        msg = msg + jnp.dot(select[3], g_ref[:, cols(k, 1)], preferred_element_type=F32)
        outbox[k] = msg.astype(BF).reshape(EXPERTS, 16, cw)
        for d in range(1, EXPERTS):
            dispatch(k, (me + d) % EXPERTS, me).start()
        rin[k, 0, me] = outbox[k, me]

    @pl.loop(0, kd + 1)
    def _(step):
        @pl.when(step < kd)
        def _():
            for d in range(1, EXPERTS):
                p = (me + d) % EXPERTS
                dispatch(step, p, p).wait_recv()
            forward(step).start()

        @pl.when(step >= 1)
        def _():
            k = step - 1
            for copy in weight_copies(k):
                copy.wait()
            forward(k).wait_recv()
            rows = jnp.dot(
                perm[...], rin[k].reshape(2 * n, cw), preferred_element_type=F32
            ).astype(BF)
            for h in range(2):
                xs = rows[h * 128 : h * 128 + 64]
                gs = rows[h * 128 + 64 : h * 128 + 128]
                acc_g[...] += jnp.dot(xs, wg[cols(k, h), :], preferred_element_type=F32)
                acc_u[...] += jnp.dot(xs, wu[cols(k, h), :], preferred_element_type=F32)
                acc_h[...] += lax.dot_general(gs, wd[:, cols(k, h)], NT, preferred_element_type=F32)

    gate, up, hidden = acc_g[...], acc_u[...], acc_h[...]
    sig = jax.nn.sigmoid(gate)
    gg[...] = (hidden * up * sig * (1.0 + gate * (1.0 - sig))).astype(BF)
    uu[...] = (hidden * gate * sig).astype(BF)

    @pl.loop(0, kr + 2)
    def _(step):
        @pl.when(step < kr)
        def _():
            for q in range(4):
                part = lax.dot_general(gg[...], wg[qcols(step, q), :], NT, preferred_element_type=F32)
                part = part + lax.dot_general(
                    uu[...], wu[qcols(step, q), :], NT, preferred_element_type=F32
                )
                own[step, q * 32 : (q + 1) * 32, :] = part[:32]
                pout[step, q * 32 : (q + 1) * 32, :] = part[32:].astype(BF)
            exchange(step).start()

        @pl.when((step >= 1) & (step < kr + 1))
        def _():
            k = step - 1
            exchange(k).wait_recv()
            total = (own[k] + pin[k].astype(F32)).astype(BF)
            rout[k] = (
                jnp.dot(perm_back[...], total, preferred_element_type=F32)
                .astype(BF)
                .reshape(EXPERTS, 16, qw)
            )
            for d in range(1, EXPERTS):
                giveback(k, (me + d) % EXPERTS, me).start()
            rret[k, me] = rout[k, me]

        @pl.when(step >= 2)
        def _():
            k = step - 2
            for d in range(1, EXPERTS):
                p = (me + d) % EXPERTS
                giveback(k, p, p).wait_recv()
            rows = rret[k].reshape(n, qw)
            for q in range(4):
                out_ref[:, qcols(k, q)] = jnp.dot(
                    coef[q], rows, preferred_element_type=F32
                ).astype(BF)

    @pl.loop(0, kd)
    def _(k):
        for d in range(1, EXPERTS):
            dispatch(k, (me + d) % EXPERTS, me).wait_send()
        forward(k).wait_send()

    @pl.loop(0, kr)
    def _(k):
        for d in range(1, EXPERTS):
            giveback(k, (me + d) % EXPERTS, me).wait_send()
        exchange(k).wait_send()


def fused(inputs_saved, out_grad, expert_ids, routing_weights, w_gate, w_up, w_down):
    tokens, width = inputs_saved.shape
    units = w_gate.shape[2]
    kd, kr = KD, KR
    cw, qw = width // 2 // kd, width // 4 // kr
    rows = 2 * EXPERTS * MOST
    n = EXPERTS * 16
    vmem = pl.BlockSpec(memory_space=pltpu.VMEM)
    hbm = pl.BlockSpec(memory_space=pl.ANY)
    dma = pltpu.SemaphoreType.DMA
    return pl.pallas_call(
        functools.partial(fused_kernel, kd, kr),
        out_shape=jax.ShapeDtypeStruct((tokens, width), BF),
        in_specs=[vmem] * 4 + [hbm] * 3,
        out_specs=vmem,
        scratch_shapes=[
            pltpu.VMEM((width, units), BF),
            pltpu.VMEM((width, units), BF),
            pltpu.VMEM((units, width), BF),
            pltpu.VMEM((kd, EXPERTS, 16, cw), BF),
            pltpu.VMEM((kd, 2, EXPERTS, 16, cw), BF),
            pltpu.VMEM((rows, units), F32),
            pltpu.VMEM((rows, units), F32),
            pltpu.VMEM((rows, units), F32),
            pltpu.VMEM((rows, units), BF),
            pltpu.VMEM((rows, units), BF),
            pltpu.VMEM((kr, n, qw), F32),
            pltpu.VMEM((kr, n, qw), BF),
            pltpu.VMEM((kr, n, qw), BF),
            pltpu.VMEM((kr, EXPERTS, 16, qw), BF),
            pltpu.VMEM((kr, EXPERTS, 16, qw), BF),
            pltpu.VMEM((4, n, tokens), BF),
            pltpu.VMEM((4, tokens, n), BF),
            pltpu.VMEM((2 * n, 2 * n), BF),
            pltpu.VMEM((n, n), BF),
            dma((3, kd, 2)),
            dma((kd, EXPERTS)),
            dma((kd, EXPERTS)),
            dma((kd,)),
            dma((kd,)),
            dma((kr,)),
            dma((kr,)),
            dma((kr, EXPERTS)),
            dma((kr, EXPERTS)),
        ],
        compiler_params=pltpu.CompilerParams(
            collective_id=0, has_side_effects=True, vmem_limit_bytes=62 * 1024 * 1024
        ),
    )(inputs_saved, out_grad, expert_ids.T, routing_weights.T, w_gate, w_up, w_down)


def fits(mesh, x_shape, w_shape):
    return (
        mesh.shape["inter"] == 2
        and mesh.shape["intra"] == 2 * EG
        and x_shape[1] % (256 * KD) == 0
        and x_shape[1] % (512 * KR) == 0
        and x_shape[0] == 128 * mesh.size
        and w_shape[2] <= 1024
    )


def solution(mesh):
    in_specs = (
        P(("rep", "inter", "intra"), None),
        P(("rep", "inter", "intra"), None),
        P(("rep", "inter", "intra"), None),
        P(("rep", "inter", "intra"), None),
        P(("inter", "intra"), None, None),
        P(("inter", "intra"), None, None),
        P(("inter", "intra"), None, None),
    )
    out_specs = P(("rep", "inter", "intra"), None)

    def run(*args):
        body = fused if fits(mesh, args[0].shape, args[4].shape) else on_device
        return jax.shard_map(
            body, mesh=mesh, in_specs=in_specs, out_specs=out_specs, check_vma=False
        )(*args)

    return run
```

```python
import functools

import jax
import jax.numpy as jnp
from jax import lax
from jax.experimental import pallas as pl
from jax.experimental.pallas import tpu as pltpu
from jax.sharding import PartitionSpec as P

EG = 4
MOST = 4
KD = 7
KR = 2


def expert_rows(rows_x, rows_grad, scales, gate_mat, up_mat, down_mat):
    gate_pre = jnp.dot(rows_x, gate_mat, preferred_element_type=jnp.float32)
    up_pre = jnp.dot(rows_x, up_mat, preferred_element_type=jnp.float32)
    hidden_raw = lax.dot_general(
        rows_grad, down_mat, (((1,), (1,)), ((), ())), preferred_element_type=jnp.float32
    )
    hidden_grad = scales.astype(jnp.float32)[:, None] * hidden_raw
    sigmoid_gate = jax.nn.sigmoid(gate_pre)
    gate_grad = (
        hidden_grad * up_pre * sigmoid_gate * (1.0 + gate_pre * (1.0 - sigmoid_gate))
    ).astype(jnp.bfloat16)
    up_grad = (hidden_grad * gate_pre * sigmoid_gate).astype(jnp.bfloat16)
    contract = (((1,), (1,)), ((), ()))
    result = lax.dot_general(gate_grad, gate_mat, contract, preferred_element_type=jnp.float32)
    result = result + lax.dot_general(up_grad, up_mat, contract, preferred_element_type=jnp.float32)
    return result.astype(jnp.bfloat16)


def on_device(inputs_saved, out_grad, expert_ids, routing_weights, w_gate, w_up, w_down):
    n_inter = lax.axis_size("inter")
    n_intra = lax.axis_size("intra")
    shard_count = n_intra // EG
    window = n_inter * EG
    width = inputs_saved.shape[1]
    token_count = inputs_saved.shape[0]
    top_count = expert_ids.shape[1]
    slot_count = MOST
    gate_mat = w_gate[0]
    up_mat = w_up[0]
    down_mat = w_down[0]
    pair_experts = expert_ids.reshape(-1)
    onehot = (pair_experts[:, None] == jnp.arange(window, dtype=jnp.int32)[None, :]).astype(
        jnp.int32
    )
    slot_rank = jnp.cumsum(onehot, axis=0) - 1
    select = onehot[None, :, :] * (
        slot_rank[None, :, :] == jnp.arange(slot_count, dtype=jnp.int32)[:, None, None]
    ).astype(jnp.int32)
    per_token = select.reshape(slot_count, token_count, top_count, window).sum(axis=2)
    chosen = per_token.transpose(2, 0, 1).reshape(window * slot_count, token_count)
    chosen_bf = chosen.astype(jnp.bfloat16)
    x_buffer = (
        jnp.dot(chosen_bf, inputs_saved, preferred_element_type=jnp.float32)
        .astype(jnp.bfloat16)
        .reshape(window, slot_count, width)
    )
    grad_buffer = (
        jnp.dot(chosen_bf, out_grad, preferred_element_type=jnp.float32)
        .astype(jnp.bfloat16)
        .reshape(window, slot_count, width)
    )
    scale_sum = jnp.sum(
        select.astype(jnp.float32) * routing_weights.reshape(-1).astype(jnp.float32)[None, :, None],
        axis=1,
    )
    scale_buffer = scale_sum.transpose(1, 0).astype(jnp.bfloat16)
    outbox = (
        jnp.repeat(x_buffer, shard_count, axis=0),
        jnp.repeat(grad_buffer, shard_count, axis=0),
        jnp.repeat(scale_buffer, shard_count, axis=0),
    )
    rows_x = lax.all_to_all(outbox[0], ("inter", "intra"), split_axis=0, concat_axis=0, tiled=True)
    leading = rows_x.shape[:-1]
    result = expert_rows(
        rows_x.reshape(-1, width),
        lax.all_to_all(
            outbox[1], ("inter", "intra"), split_axis=0, concat_axis=0, tiled=True
        ).reshape(-1, width),
        lax.all_to_all(
            outbox[2], ("inter", "intra"), split_axis=0, concat_axis=0, tiled=True
        ).reshape(-1),
        gate_mat,
        up_mat,
        down_mat,
    )
    partial_rows = result.reshape(leading + (width,))
    returned = lax.all_to_all(
        partial_rows, ("inter", "intra"), split_axis=0, concat_axis=0, tiled=True
    )
    summed = (
        returned.astype(jnp.float32).reshape(window, shard_count, slot_count, width).sum(axis=1)
    )
    gathered = jnp.dot(
        chosen.astype(jnp.float32).T,
        summed.reshape(window * slot_count, width),
        precision=lax.Precision.HIGHEST,
        preferred_element_type=jnp.float32,
    )
    return gathered.astype(jnp.bfloat16)


MESH = pl.DeviceIdType.MESH
BF = jnp.bfloat16
F32 = jnp.float32
EXPERTS = 8
NT = (((1,), (1,)), ((), ()))


def iota(shape, dim):
    return lax.broadcasted_iota(jnp.int32, shape, dim)


def fused_kernel(
    kd, kr, x_ref, g_ref, ids_ref, rw_ref, wg_hbm, wu_hbm, wd_hbm, out_ref,
    wg, wu, wd, outbox, rin, acc_g, acc_u, acc_h, gg, uu, own, pout, pin, rout, rret,
    select, coef, perm, perm_back,
    w_sem, send_sem, recv_sem, fsend, frecv, psend, precv, rsend, rrecv,
):
    tokens, width = x_ref.shape
    half, quarter = width // 2, width // 4
    cw, qw = half // kd, quarter // kr
    rep, core, pos = lax.axis_index("rep"), lax.axis_index("inter"), lax.axis_index("intra")
    z, y = pos // 2, pos % 2
    me = core * EG + z
    partner = (rep, core, z * 2 + 1 - y)

    def peer(e):
        return (rep, e // EG, (e % EG) * 2 + y)

    barrier = pltpu.get_barrier_semaphore()
    for d in range(1, EXPERTS):
        pl.semaphore_signal(barrier, inc=1, device_id=peer((me + d) % EXPERTS), device_id_type=MESH)
    pl.semaphore_signal(barrier, inc=1, device_id=partner, device_id_type=MESH)

    def cols(k, h):
        return pl.ds(pl.multiple_of(h * half + k * cw, 128), cw)

    def qcols(k, q):
        return pl.ds(pl.multiple_of(q * quarter + k * qw, 128), qw)

    def weight_copies(k):
        res = []
        for h in range(2):
            c = cols(k, h)
            res.append(pltpu.make_async_copy(wg_hbm.at[0, c, :], wg.at[c, :], w_sem.at[0, k, h]))
            res.append(pltpu.make_async_copy(wu_hbm.at[0, c, :], wu.at[c, :], w_sem.at[1, k, h]))
            res.append(pltpu.make_async_copy(wd_hbm.at[0, :, c], wd.at[:, c], w_sem.at[2, k, h]))
        return res

    @pl.loop(0, kd)
    def _(k):
        for copy in weight_copies(k):
            copy.start()

    n = EXPERTS * 16
    row = iota((n, tokens), 0)
    expert, place = row // 16, row % 4
    present = jnp.zeros((n, tokens), F32)
    weight = jnp.zeros((n, tokens), F32)
    ids = ids_ref[...]
    rw = rw_ref[...].astype(F32)
    for t in range(ids.shape[0]):
        hit = (ids[t : t + 1, :] == expert).astype(F32)
        present = present + hit
        weight = weight + hit * rw[t : t + 1, :]
    upper = (iota((tokens, tokens), 0) < iota((tokens, tokens), 1)).astype(F32).astype(BF)
    rank = jnp.dot(present.astype(BF), upper, preferred_element_type=F32)
    chosen = jnp.where(rank == place.astype(F32), present, 0.0)
    coef_all = (chosen * weight).T
    col = iota((tokens, n), 1)
    for q in range(4):
        coef[q] = jnp.where((col % 16) // 4 == q, coef_all, 0.0).astype(BF)
    for j in range(4):
        select[j] = jnp.where((row % 16) // 4 == j, chosen, 0.0).astype(BF)
    o, c = iota((2 * n, 2 * n), 0), iota((2 * n, 2 * n), 1)
    source = ((o // 32) % 2) * 128 + ((o // 4) % 8) * 16 + (o // 128) * 8 + ((o // 64) % 2) * 4 + o % 4
    perm[...] = (c == source).astype(F32).astype(BF)
    o, c = iota((n, n), 0), iota((n, n), 1)
    perm_back[...] = (c == ((o // 4) % 4) * 32 + (o // 16) * 4 + o % 4).astype(F32).astype(BF)

    acc_g[...] = jnp.zeros_like(acc_g)
    acc_u[...] = jnp.zeros_like(acc_u)
    acc_h[...] = jnp.zeros_like(acc_h)

    def dispatch(k, e, slot):
        return pltpu.make_async_remote_copy(
            src_ref=outbox.at[k, e], dst_ref=rin.at[k, 0, slot],
            send_sem=send_sem.at[k, e], recv_sem=recv_sem.at[k, slot],
            device_id=peer(e), device_id_type=MESH,
        )

    def forward(k):
        return pltpu.make_async_remote_copy(
            src_ref=rin.at[k, 0], dst_ref=rin.at[k, 1],
            send_sem=fsend.at[k], recv_sem=frecv.at[k],
            device_id=partner, device_id_type=MESH,
        )

    def exchange(k, i):
        span = pl.ds(i * 64, 64)
        return pltpu.make_async_remote_copy(
            src_ref=pout.at[k, span], dst_ref=pin.at[k, span],
            send_sem=psend.at[k, i], recv_sem=precv.at[k, i],
            device_id=partner, device_id_type=MESH,
        )

    def giveback(k, e, slot):
        return pltpu.make_async_remote_copy(
            src_ref=rout.at[k, e], dst_ref=rret.at[k, slot],
            send_sem=rsend.at[k, e], recv_sem=rrecv.at[k, slot],
            device_id=peer(e), device_id_type=MESH,
        )

    pl.semaphore_wait(barrier, EXPERTS)

    @pl.loop(0, kd)
    def _(k):
        msg = jnp.dot(select[0], x_ref[:, cols(k, 0)], preferred_element_type=F32)
        msg = msg + jnp.dot(select[1], g_ref[:, cols(k, 0)], preferred_element_type=F32)
        msg = msg + jnp.dot(select[2], x_ref[:, cols(k, 1)], preferred_element_type=F32)
        msg = msg + jnp.dot(select[3], g_ref[:, cols(k, 1)], preferred_element_type=F32)
        outbox[k] = msg.astype(BF).reshape(EXPERTS, 16, cw)
        for d in range(1, EXPERTS):
            dispatch(k, (me + d) % EXPERTS, me).start()
        rin[k, 0, me] = outbox[k, me]

    @pl.loop(0, kd + 1)
    def _(step):
        @pl.when(step < kd)
        def _():
            for d in range(1, EXPERTS):
                p = (me + d) % EXPERTS
                dispatch(step, p, p).wait_recv()
            forward(step).start()

        @pl.when(step >= 1)
        def _():
            k = step - 1
            for copy in weight_copies(k):
                copy.wait()
            forward(k).wait_recv()
            rows = jnp.dot(
                perm[...], rin[k].reshape(2 * n, cw), preferred_element_type=F32
            ).astype(BF)
            for h in range(2):
                xs = rows[h * 128 : h * 128 + 64]
                gs = rows[h * 128 + 64 : h * 128 + 128]
                acc_g[...] += jnp.dot(xs, wg[cols(k, h), :], preferred_element_type=F32)
                acc_u[...] += jnp.dot(xs, wu[cols(k, h), :], preferred_element_type=F32)
                acc_h[...] += lax.dot_general(gs, wd[:, cols(k, h)], NT, preferred_element_type=F32)

    gate, up, hidden = acc_g[...], acc_u[...], acc_h[...]
    sig = jax.nn.sigmoid(gate)
    gg[...] = (hidden * up * sig * (1.0 + gate * (1.0 - sig))).astype(BF)
    uu[...] = (hidden * gate * sig).astype(BF)

    def give(k):
        exchange(k, 0).wait_recv()
        exchange(k, 1).wait_recv()
        total = (own[k] + pin[k].astype(F32)).astype(BF)
        rout[k] = (
            jnp.dot(perm_back[...], total, preferred_element_type=F32)
            .astype(BF)
            .reshape(EXPERTS, 16, qw)
        )
        for d in range(1, EXPERTS):
            giveback(k, (me + d) % EXPERTS, me).start()
        rret[k, me] = rout[k, me]

    @pl.loop(0, kr)
    def _(step):
        for i in range(2):
            for q in (2 * i, 2 * i + 1):
                part = lax.dot_general(gg[...], wg[qcols(step, q), :], NT, preferred_element_type=F32)
                part = part + lax.dot_general(
                    uu[...], wu[qcols(step, q), :], NT, preferred_element_type=F32
                )
                own[step, q * 32 : (q + 1) * 32, :] = part[:32]
                pout[step, q * 32 : (q + 1) * 32, :] = part[32:].astype(BF)
            exchange(step, i).start()
            if i == 0:
                @pl.when(step >= 1)
                def _():
                    give(step - 1)

    give(kr - 1)

    @pl.loop(0, kr)
    def _(k):
        for d in range(1, EXPERTS):
            p = (me + d) % EXPERTS
            giveback(k, p, p).wait_recv()
        rows = rret[k].reshape(n, qw)
        for q in range(4):
            out_ref[:, qcols(k, q)] = jnp.dot(
                coef[q], rows, preferred_element_type=F32
            ).astype(BF)

    @pl.loop(0, kd)
    def _(k):
        for d in range(1, EXPERTS):
            dispatch(k, (me + d) % EXPERTS, me).wait_send()
        forward(k).wait_send()

    @pl.loop(0, kr)
    def _(k):
        for d in range(1, EXPERTS):
            giveback(k, (me + d) % EXPERTS, me).wait_send()
        exchange(k, 0).wait_send()
        exchange(k, 1).wait_send()


def fused(inputs_saved, out_grad, expert_ids, routing_weights, w_gate, w_up, w_down):
    tokens, width = inputs_saved.shape
    units = w_gate.shape[2]
    kd, kr = KD, KR
    cw, qw = width // 2 // kd, width // 4 // kr
    rows = 2 * EXPERTS * MOST
    n = EXPERTS * 16
    vmem = pl.BlockSpec(memory_space=pltpu.VMEM)
    hbm = pl.BlockSpec(memory_space=pl.ANY)
    dma = pltpu.SemaphoreType.DMA
    return pl.pallas_call(
        functools.partial(fused_kernel, kd, kr),
        out_shape=jax.ShapeDtypeStruct((tokens, width), BF),
        in_specs=[vmem] * 4 + [hbm] * 3,
        out_specs=vmem,
        scratch_shapes=[
            pltpu.VMEM((width, units), BF),
            pltpu.VMEM((width, units), BF),
            pltpu.VMEM((units, width), BF),
            pltpu.VMEM((kd, EXPERTS, 16, cw), BF),
            pltpu.VMEM((kd, 2, EXPERTS, 16, cw), BF),
            pltpu.VMEM((rows, units), F32),
            pltpu.VMEM((rows, units), F32),
            pltpu.VMEM((rows, units), F32),
            pltpu.VMEM((rows, units), BF),
            pltpu.VMEM((rows, units), BF),
            pltpu.VMEM((kr, n, qw), F32),
            pltpu.VMEM((kr, n, qw), BF),
            pltpu.VMEM((kr, n, qw), BF),
            pltpu.VMEM((kr, EXPERTS, 16, qw), BF),
            pltpu.VMEM((kr, EXPERTS, 16, qw), BF),
            pltpu.VMEM((4, n, tokens), BF),
            pltpu.VMEM((4, tokens, n), BF),
            pltpu.VMEM((2 * n, 2 * n), BF),
            pltpu.VMEM((n, n), BF),
            dma((3, kd, 2)),
            dma((kd, EXPERTS)),
            dma((kd, EXPERTS)),
            dma((kd,)),
            dma((kd,)),
            dma((kr, 2)),
            dma((kr, 2)),
            dma((kr, EXPERTS)),
            dma((kr, EXPERTS)),
        ],
        compiler_params=pltpu.CompilerParams(
            collective_id=0, has_side_effects=True, vmem_limit_bytes=62 * 1024 * 1024
        ),
    )(inputs_saved, out_grad, expert_ids.T, routing_weights.T, w_gate, w_up, w_down)


def fits(mesh, x_shape, w_shape):
    return (
        mesh.shape["inter"] == 2
        and mesh.shape["intra"] == 2 * EG
        and x_shape[1] % (256 * KD) == 0
        and x_shape[1] % (512 * KR) == 0
        and x_shape[0] == 128 * mesh.size
        and w_shape[2] <= 1024
    )


def solution(mesh):
    in_specs = (
        P(("rep", "inter", "intra"), None),
        P(("rep", "inter", "intra"), None),
        P(("rep", "inter", "intra"), None),
        P(("rep", "inter", "intra"), None),
        P(("inter", "intra"), None, None),
        P(("inter", "intra"), None, None),
        P(("inter", "intra"), None, None),
    )
    out_specs = P(("rep", "inter", "intra"), None)

    def run(*args):
        body = fused if fits(mesh, args[0].shape, args[4].shape) else on_device
        return jax.shard_map(
            body, mesh=mesh, in_specs=in_specs, out_specs=out_specs, check_vma=False
        )(*args)

    return run
```

```python
import functools

import jax
import jax.numpy as jnp
from jax import lax
from jax.experimental import pallas as pl
from jax.experimental.pallas import tpu as pltpu
from jax.sharding import PartitionSpec as P

EG = 4
MOST = 4
KD = 7
KR = 2


def expert_rows(rows_x, rows_grad, scales, gate_mat, up_mat, down_mat):
    gate_pre = jnp.dot(rows_x, gate_mat, preferred_element_type=jnp.float32)
    up_pre = jnp.dot(rows_x, up_mat, preferred_element_type=jnp.float32)
    hidden_raw = lax.dot_general(
        rows_grad, down_mat, (((1,), (1,)), ((), ())), preferred_element_type=jnp.float32
    )
    hidden_grad = scales.astype(jnp.float32)[:, None] * hidden_raw
    sigmoid_gate = jax.nn.sigmoid(gate_pre)
    gate_grad = (
        hidden_grad * up_pre * sigmoid_gate * (1.0 + gate_pre * (1.0 - sigmoid_gate))
    ).astype(jnp.bfloat16)
    up_grad = (hidden_grad * gate_pre * sigmoid_gate).astype(jnp.bfloat16)
    contract = (((1,), (1,)), ((), ()))
    result = lax.dot_general(gate_grad, gate_mat, contract, preferred_element_type=jnp.float32)
    result = result + lax.dot_general(up_grad, up_mat, contract, preferred_element_type=jnp.float32)
    return result.astype(jnp.bfloat16)


def on_device(inputs_saved, out_grad, expert_ids, routing_weights, w_gate, w_up, w_down):
    n_inter = lax.axis_size("inter")
    n_intra = lax.axis_size("intra")
    shard_count = n_intra // EG
    window = n_inter * EG
    width = inputs_saved.shape[1]
    token_count = inputs_saved.shape[0]
    top_count = expert_ids.shape[1]
    slot_count = MOST
    gate_mat = w_gate[0]
    up_mat = w_up[0]
    down_mat = w_down[0]
    pair_experts = expert_ids.reshape(-1)
    onehot = (pair_experts[:, None] == jnp.arange(window, dtype=jnp.int32)[None, :]).astype(
        jnp.int32
    )
    slot_rank = jnp.cumsum(onehot, axis=0) - 1
    select = onehot[None, :, :] * (
        slot_rank[None, :, :] == jnp.arange(slot_count, dtype=jnp.int32)[:, None, None]
    ).astype(jnp.int32)
    per_token = select.reshape(slot_count, token_count, top_count, window).sum(axis=2)
    chosen = per_token.transpose(2, 0, 1).reshape(window * slot_count, token_count)
    chosen_bf = chosen.astype(jnp.bfloat16)
    x_buffer = (
        jnp.dot(chosen_bf, inputs_saved, preferred_element_type=jnp.float32)
        .astype(jnp.bfloat16)
        .reshape(window, slot_count, width)
    )
    grad_buffer = (
        jnp.dot(chosen_bf, out_grad, preferred_element_type=jnp.float32)
        .astype(jnp.bfloat16)
        .reshape(window, slot_count, width)
    )
    scale_sum = jnp.sum(
        select.astype(jnp.float32) * routing_weights.reshape(-1).astype(jnp.float32)[None, :, None],
        axis=1,
    )
    scale_buffer = scale_sum.transpose(1, 0).astype(jnp.bfloat16)
    outbox = (
        jnp.repeat(x_buffer, shard_count, axis=0),
        jnp.repeat(grad_buffer, shard_count, axis=0),
        jnp.repeat(scale_buffer, shard_count, axis=0),
    )
    rows_x = lax.all_to_all(outbox[0], ("inter", "intra"), split_axis=0, concat_axis=0, tiled=True)
    leading = rows_x.shape[:-1]
    result = expert_rows(
        rows_x.reshape(-1, width),
        lax.all_to_all(
            outbox[1], ("inter", "intra"), split_axis=0, concat_axis=0, tiled=True
        ).reshape(-1, width),
        lax.all_to_all(
            outbox[2], ("inter", "intra"), split_axis=0, concat_axis=0, tiled=True
        ).reshape(-1),
        gate_mat,
        up_mat,
        down_mat,
    )
    partial_rows = result.reshape(leading + (width,))
    returned = lax.all_to_all(
        partial_rows, ("inter", "intra"), split_axis=0, concat_axis=0, tiled=True
    )
    summed = (
        returned.astype(jnp.float32).reshape(window, shard_count, slot_count, width).sum(axis=1)
    )
    gathered = jnp.dot(
        chosen.astype(jnp.float32).T,
        summed.reshape(window * slot_count, width),
        precision=lax.Precision.HIGHEST,
        preferred_element_type=jnp.float32,
    )
    return gathered.astype(jnp.bfloat16)


MESH = pl.DeviceIdType.MESH
BF = jnp.bfloat16
F32 = jnp.float32
EXPERTS = 8
NT = (((1,), (1,)), ((), ()))


def iota(shape, dim):
    return lax.broadcasted_iota(jnp.int32, shape, dim)


def fused_kernel(
    kd, kr, x_ref, g_ref, ids_ref, rw_ref, wg_hbm, wu_hbm, wd_hbm, out_ref,
    wg, wu, wd, outbox, rin, acc_g, acc_u, acc_h, gg, uu, own, pout, pin, rout, rret,
    select, coef, perm, perm_back,
    w_sem, send_sem, recv_sem, fsend, frecv, psend, precv, rsend, rrecv,
):
    tokens, width = x_ref.shape
    half, quarter = width // 2, width // 4
    cw, qw = half // kd, quarter // kr
    rep, core, pos = lax.axis_index("rep"), lax.axis_index("inter"), lax.axis_index("intra")
    z, y = pos // 2, pos % 2
    me = core * EG + z
    partner = (rep, core, z * 2 + 1 - y)

    def peer(e):
        return (rep, e // EG, (e % EG) * 2 + y)

    barrier = pltpu.get_barrier_semaphore()
    for d in range(1, EXPERTS):
        pl.semaphore_signal(barrier, inc=1, device_id=peer((me + d) % EXPERTS), device_id_type=MESH)
    pl.semaphore_signal(barrier, inc=1, device_id=partner, device_id_type=MESH)

    def cols(k, h):
        return pl.ds(pl.multiple_of(h * half + k * cw, 128), cw)

    def qcols(k, q):
        return pl.ds(pl.multiple_of(q * quarter + k * qw, 128), qw)

    def weight_copies(k):
        res = []
        for h in range(2):
            c = cols(k, h)
            res.append(pltpu.make_async_copy(wg_hbm.at[0, c, :], wg.at[c, :], w_sem.at[0, k, h]))
            res.append(pltpu.make_async_copy(wu_hbm.at[0, c, :], wu.at[c, :], w_sem.at[1, k, h]))
            res.append(pltpu.make_async_copy(wd_hbm.at[0, :, c], wd.at[:, c], w_sem.at[2, k, h]))
        return res

    n = EXPERTS * 16
    row = iota((n, tokens), 0)
    expert, place = row // 16, row % 4
    present = jnp.zeros((n, tokens), F32)
    weight = jnp.zeros((n, tokens), F32)
    ids = ids_ref[...]
    rw = rw_ref[...].astype(F32)
    for t in range(ids.shape[0]):
        hit = (ids[t : t + 1, :] == expert).astype(F32)
        present = present + hit
        weight = weight + hit * rw[t : t + 1, :]
    upper = (iota((tokens, tokens), 0) < iota((tokens, tokens), 1)).astype(F32).astype(BF)
    rank = jnp.dot(present.astype(BF), upper, preferred_element_type=F32)
    chosen = jnp.where(rank == place.astype(F32), present, 0.0)
    coef_all = (chosen * weight).T
    col = iota((tokens, n), 1)
    for q in range(4):
        coef[q] = jnp.where((col % 16) // 4 == q, coef_all, 0.0).astype(BF)
    for j in range(4):
        select[j] = jnp.where((row % 16) // 4 == j, chosen, 0.0).astype(BF)
    o, c = iota((2 * n, 2 * n), 0), iota((2 * n, 2 * n), 1)
    source = ((o // 32) % 2) * 128 + ((o // 4) % 8) * 16 + (o // 128) * 8 + ((o // 64) % 2) * 4 + o % 4
    perm[...] = (c == source).astype(F32).astype(BF)
    o, c = iota((n, n), 0), iota((n, n), 1)
    perm_back[...] = (c == ((o // 4) % 4) * 32 + (o // 16) * 4 + o % 4).astype(F32).astype(BF)

    acc_g[...] = jnp.zeros_like(acc_g)
    acc_u[...] = jnp.zeros_like(acc_u)
    acc_h[...] = jnp.zeros_like(acc_h)

    def dispatch(k, e, slot):
        return pltpu.make_async_remote_copy(
            src_ref=outbox.at[k, e], dst_ref=rin.at[k, 0, slot],
            send_sem=send_sem.at[k, e], recv_sem=recv_sem.at[k, slot],
            device_id=peer(e), device_id_type=MESH,
        )

    def forward(k):
        return pltpu.make_async_remote_copy(
            src_ref=rin.at[k, 0], dst_ref=rin.at[k, 1],
            send_sem=fsend.at[k], recv_sem=frecv.at[k],
            device_id=partner, device_id_type=MESH,
        )

    def exchange(k, i):
        span = pl.ds(i * 64, 64)
        return pltpu.make_async_remote_copy(
            src_ref=pout.at[k, span], dst_ref=pin.at[k, span],
            send_sem=psend.at[k, i], recv_sem=precv.at[k, i],
            device_id=partner, device_id_type=MESH,
        )

    def giveback(k, e, slot):
        return pltpu.make_async_remote_copy(
            src_ref=rout.at[k, e], dst_ref=rret.at[k, slot],
            send_sem=rsend.at[k, e], recv_sem=rrecv.at[k, slot],
            device_id=peer(e), device_id_type=MESH,
        )

    pl.semaphore_wait(barrier, EXPERTS)

    @pl.loop(0, kd)
    def _(k):
        msg = jnp.dot(select[0], x_ref[:, cols(k, 0)], preferred_element_type=F32)
        msg = msg + jnp.dot(select[1], g_ref[:, cols(k, 0)], preferred_element_type=F32)
        msg = msg + jnp.dot(select[2], x_ref[:, cols(k, 1)], preferred_element_type=F32)
        msg = msg + jnp.dot(select[3], g_ref[:, cols(k, 1)], preferred_element_type=F32)
        outbox[k] = msg.astype(BF).reshape(EXPERTS, 16, cw)
        for d in range(1, EXPERTS):
            dispatch(k, (me + d) % EXPERTS, me).start()
        rin[k, 0, me] = outbox[k, me]
        for copy in weight_copies(k):
            copy.start()

    @pl.loop(0, kd + 1)
    def _(step):
        @pl.when(step < kd)
        def _():
            for d in range(1, EXPERTS):
                p = (me + d) % EXPERTS
                dispatch(step, p, p).wait_recv()
            forward(step).start()

        @pl.when(step >= 1)
        def _():
            k = step - 1
            for copy in weight_copies(k):
                copy.wait()
            forward(k).wait_recv()
            rows = jnp.dot(
                perm[...], rin[k].reshape(2 * n, cw), preferred_element_type=F32
            ).astype(BF)
            for h in range(2):
                xs = rows[h * 128 : h * 128 + 64]
                gs = rows[h * 128 + 64 : h * 128 + 128]
                acc_g[...] += jnp.dot(xs, wg[cols(k, h), :], preferred_element_type=F32)
                acc_u[...] += jnp.dot(xs, wu[cols(k, h), :], preferred_element_type=F32)
                acc_h[...] += lax.dot_general(gs, wd[:, cols(k, h)], NT, preferred_element_type=F32)

    gate, up, hidden = acc_g[...], acc_u[...], acc_h[...]
    sig = jax.nn.sigmoid(gate)
    gg[...] = (hidden * up * sig * (1.0 + gate * (1.0 - sig))).astype(BF)
    uu[...] = (hidden * gate * sig).astype(BF)

    def give(k):
        exchange(k, 0).wait_recv()
        exchange(k, 1).wait_recv()
        total = (own[k] + pin[k].astype(F32)).astype(BF)
        rout[k] = (
            jnp.dot(perm_back[...], total, preferred_element_type=F32)
            .astype(BF)
            .reshape(EXPERTS, 16, qw)
        )
        for d in range(1, EXPERTS):
            giveback(k, (me + d) % EXPERTS, me).start()
        rret[k, me] = rout[k, me]

    @pl.loop(0, kr)
    def _(step):
        for i in range(2):
            for q in (2 * i, 2 * i + 1):
                part = lax.dot_general(gg[...], wg[qcols(step, q), :], NT, preferred_element_type=F32)
                part = part + lax.dot_general(
                    uu[...], wu[qcols(step, q), :], NT, preferred_element_type=F32
                )
                own[step, q * 32 : (q + 1) * 32, :] = part[:32]
                pout[step, q * 32 : (q + 1) * 32, :] = part[32:].astype(BF)
            exchange(step, i).start()
            if i == 0:
                @pl.when(step >= 1)
                def _():
                    give(step - 1)

    give(kr - 1)

    @pl.loop(0, kr)
    def _(k):
        for d in range(1, EXPERTS):
            p = (me + d) % EXPERTS
            giveback(k, p, p).wait_recv()
        rows = rret[k].reshape(n, qw)
        for q in range(4):
            out_ref[:, qcols(k, q)] = jnp.dot(
                coef[q], rows, preferred_element_type=F32
            ).astype(BF)

    @pl.loop(0, kd)
    def _(k):
        for d in range(1, EXPERTS):
            dispatch(k, (me + d) % EXPERTS, me).wait_send()
        forward(k).wait_send()

    @pl.loop(0, kr)
    def _(k):
        for d in range(1, EXPERTS):
            giveback(k, (me + d) % EXPERTS, me).wait_send()
        exchange(k, 0).wait_send()
        exchange(k, 1).wait_send()


def fused(inputs_saved, out_grad, expert_ids, routing_weights, w_gate, w_up, w_down):
    tokens, width = inputs_saved.shape
    units = w_gate.shape[2]
    kd, kr = KD, KR
    cw, qw = width // 2 // kd, width // 4 // kr
    rows = 2 * EXPERTS * MOST
    n = EXPERTS * 16
    vmem = pl.BlockSpec(memory_space=pltpu.VMEM)
    hbm = pl.BlockSpec(memory_space=pl.ANY)
    dma = pltpu.SemaphoreType.DMA
    return pl.pallas_call(
        functools.partial(fused_kernel, kd, kr),
        out_shape=jax.ShapeDtypeStruct((tokens, width), BF),
        in_specs=[vmem] * 4 + [hbm] * 3,
        out_specs=vmem,
        scratch_shapes=[
            pltpu.VMEM((width, units), BF),
            pltpu.VMEM((width, units), BF),
            pltpu.VMEM((units, width), BF),
            pltpu.VMEM((kd, EXPERTS, 16, cw), BF),
            pltpu.VMEM((kd, 2, EXPERTS, 16, cw), BF),
            pltpu.VMEM((rows, units), F32),
            pltpu.VMEM((rows, units), F32),
            pltpu.VMEM((rows, units), F32),
            pltpu.VMEM((rows, units), BF),
            pltpu.VMEM((rows, units), BF),
            pltpu.VMEM((kr, n, qw), F32),
            pltpu.VMEM((kr, n, qw), BF),
            pltpu.VMEM((kr, n, qw), BF),
            pltpu.VMEM((kr, EXPERTS, 16, qw), BF),
            pltpu.VMEM((kr, EXPERTS, 16, qw), BF),
            pltpu.VMEM((4, n, tokens), BF),
            pltpu.VMEM((4, tokens, n), BF),
            pltpu.VMEM((2 * n, 2 * n), BF),
            pltpu.VMEM((n, n), BF),
            dma((3, kd, 2)),
            dma((kd, EXPERTS)),
            dma((kd, EXPERTS)),
            dma((kd,)),
            dma((kd,)),
            dma((kr, 2)),
            dma((kr, 2)),
            dma((kr, EXPERTS)),
            dma((kr, EXPERTS)),
        ],
        compiler_params=pltpu.CompilerParams(
            collective_id=0, has_side_effects=True, vmem_limit_bytes=62 * 1024 * 1024
        ),
    )(inputs_saved, out_grad, expert_ids.T, routing_weights.T, w_gate, w_up, w_down)


def fits(mesh, x_shape, w_shape):
    return (
        mesh.shape["inter"] == 2
        and mesh.shape["intra"] == 2 * EG
        and x_shape[1] % (256 * KD) == 0
        and x_shape[1] % (512 * KR) == 0
        and x_shape[0] == 128 * mesh.size
        and w_shape[2] <= 1024
    )


def solution(mesh):
    in_specs = (
        P(("rep", "inter", "intra"), None),
        P(("rep", "inter", "intra"), None),
        P(("rep", "inter", "intra"), None),
        P(("rep", "inter", "intra"), None),
        P(("inter", "intra"), None, None),
        P(("inter", "intra"), None, None),
        P(("inter", "intra"), None, None),
    )
    out_specs = P(("rep", "inter", "intra"), None)

    def run(*args):
        body = fused if fits(mesh, args[0].shape, args[4].shape) else on_device
        return jax.shard_map(
            body, mesh=mesh, in_specs=in_specs, out_specs=out_specs, check_vma=False
        )(*args)

    return run
```
